256 devices in a mesh: leaf: 8 (over y, core), row: 4 (over z_hi), col: 8 (over z_lo, x).
Axes of the slice: x: 4, y: 4, z: 8 (z_hi: 4, z_lo: 2; z = z_hi * 2 + z_lo), core: 2. Of those that a mesh axis runs over, the one named last changes fastest.
Arguments:
- child_blocks: bfloat16 [8, 8192, 8192], P('leaf', None, ('row', 'col')), may hold values from -6 to 6
- child_map: int32 [8, 64], replicated, may hold values from 0 to 63, each once within a row
- merged_map: int32 [4, 60], replicated, may hold values from 0 to 63, as said below
- pivots_one: bfloat16 [4, 2, 256, 256], replicated, may hold values from -0.0234375 to 0.0234375
- pivots_two: bfloat16 [2, 2, 256, 256], replicated, may hold values from -0.015625 to 0.015625
Outputs:
- grand_front: bfloat16 [32, 8, 64, 8192], P(('row', 'col'), 'leaf')
The draws below stay inside these ranges and needn't reach their ends.
Inputs may be any that keep to these rules, and one draw needn't show every extreme that they name: `child_map`: each row orders all 64 block numbers of a first-level front. `merged_map`: the entries of a row are distinct block numbers of a second-level front.
All inputs are finite; a program needn't handle non-finite values.
Results may differ from the reference program's by a relative error of at most 0.017.
Values may be sent and summed in bfloat16 or wider, within the bound.
No kernel may reach another device: no remote copies, remote signals or barrier semaphores. Data moves between devices by JAX's collectives and lax.ppermute only.
A program may use at most 64 MiB of HBM per device.

```python
import jax
import jax.numpy as jnp

FRONT = 8192
BLOCK = 128
PANEL = 256
NB = 64
KEPT = 60
PAIRS = 4
QUADS = 2
N_LEAF = 8
N_ROW = 4
N_COL = 8


def draw_merged_map(key, part):
    key = jax.random.fold_in(key, 7)

    def one_row(row_key):
        first_key, second_key = jax.random.split(row_key)
        middle = (jax.random.permutation(first_key, NB - 2) + 1).astype(jnp.int32)
        chosen = jnp.concatenate([jnp.array([0, NB - 1], dtype=jnp.int32), middle[:KEPT - 2]])
        return chosen[jax.random.permutation(second_key, KEPT)]
    return jax.vmap(one_row)(jax.random.split(key, PAIRS))


def shard_levels(own_key, extent, pieces, smallest, top_value):
    level = 1.0
    for position, shards_of in pieces:
        heights = jax.random.uniform(jax.random.fold_in(jax.random.fold_in(own_key, 6), position), (shards_of,), jnp.float32, smallest / len(pieces), top_value / len(pieces))
        level = level * jnp.repeat(jnp.exp(heights), extent[position] // shards_of).reshape((-1,) + (1,) * (len(extent) - 1 - position))
    return level


def scatter_about(stream_key, shape, deviation, limit, cuts=(), kind=jnp.bfloat16):
    entries = deviation * jax.random.normal(stream_key, shape, jnp.float32)
    if cuts:
        entries = entries * shard_levels(stream_key, shape, cuts, -0.22, 0.18)
    return jnp.clip(entries, -limit, limit).astype(kind)


def setup_inputs(seed: int = 0) -> dict:
    key_of = jax.random.split(jax.random.key(seed), 6)
    child_blocks = scatter_about(key_of[0], (N_LEAF, FRONT, FRONT), 1.0, 6.0, ((0, 8), (2, 32)))
    child_map = jax.vmap(lambda own: jax.random.permutation(own, NB))(jax.random.split(key_of[1], N_LEAF)).reshape((N_LEAF, NB)).astype(jnp.int32)
    merged_map = draw_merged_map(jax.random.fold_in(key_of[5], 71), 0)
    pivots_one = scatter_about(key_of[3], (PAIRS, 2, PANEL, PANEL), (0.4 / PANEL), 0.0234375)
    pivots_two = scatter_about(key_of[4], (QUADS, 2, PANEL, PANEL), (0.3 / PANEL), 0.015625)
    return {"child_blocks": child_blocks, "child_map": child_map, "merged_map": merged_map, "pivots_one": pivots_one, "pivots_two": pivots_two}


def source_blocks(mapping, offset, block_count):
    target = jnp.arange(block_count, dtype=jnp.int32)
    matches = mapping[None, :] == target[:, None]
    present = jnp.any(matches, axis=1)
    anchor = jnp.arange(mapping.shape[0], dtype=jnp.int32) + offset
    source = jnp.sum(jnp.where(matches, anchor[None, :], 0), axis=1).astype(jnp.int32)
    return source, present


def take_blocks(matrix, source, present, split_axis):
    block_count = source.shape[0]
    if split_axis == 0:
        shaped = matrix.reshape(block_count, BLOCK, matrix.shape[1])
        picked = jnp.take(shaped, source, axis=0)
        picked = jnp.where(present[:, None, None], picked, jnp.zeros_like(picked))
    else:
        shaped = matrix.reshape(matrix.shape[0], block_count, BLOCK)
        picked = jnp.take(shaped, source, axis=1)
        picked = jnp.where(present[None, :, None], picked, jnp.zeros_like(picked))
    return picked.reshape(matrix.shape)


def extend_front(matrix, mapping, offset):
    source, present = source_blocks(mapping, offset, FRONT // BLOCK)
    row_moved = take_blocks(matrix, source, present, 0)
    return take_blocks(row_moved, source, present, 1)


def eliminate(front_matrix, pivots):
    for panel_index in range(2):
        columns = front_matrix[:, panel_index * PANEL:(panel_index + 1) * PANEL]
        lower_part = jnp.dot(columns, pivots[panel_index], preferred_element_type=jnp.float32).astype(jnp.bfloat16)
        update = jnp.dot(lower_part, columns.T, preferred_element_type=jnp.float32)
        front_matrix = (front_matrix.astype(jnp.float32) - update).astype(jnp.bfloat16)
    return front_matrix


def reference(child_blocks, child_map, merged_map, pivots_one, pivots_two):
    kept_offset = 2 * PANEL // BLOCK
    level_one = []
    for pair_index in range(N_LEAF // 2):
        summed = extend_front(child_blocks[2 * pair_index], child_map[2 * pair_index], 0).astype(jnp.float32)
        summed = summed + extend_front(child_blocks[2 * pair_index + 1], child_map[2 * pair_index + 1], 0).astype(jnp.float32)
        level_one.append(eliminate(summed.astype(jnp.bfloat16), pivots_one[pair_index]))
    finals = []
    for quad_index in range(N_LEAF // 4):
        summed = extend_front(level_one[2 * quad_index], merged_map[2 * quad_index], kept_offset).astype(jnp.float32)
        summed = summed + extend_front(level_one[2 * quad_index + 1], merged_map[2 * quad_index + 1], kept_offset).astype(jnp.float32)
        finals.append(eliminate(summed.astype(jnp.bfloat16), pivots_two[quad_index]))
    slice_rows = FRONT // (4 * N_ROW * N_COL)
    stacked = jnp.stack(finals).reshape(N_LEAF // 4, N_ROW * N_COL, 4, slice_rows, FRONT)
    return jnp.transpose(stacked, (1, 0, 2, 3, 4)).reshape(N_ROW * N_COL, N_LEAF, slice_rows, FRONT)
```

```python
import jax
import jax.numpy as jnp
from jax import lax
from jax.experimental import pallas as pl
from jax.experimental.pallas import tpu as pltpu
from jax.sharding import Mesh, PartitionSpec as P

BLOCK = 128
PANEL = 256
NB = 64
NZ = 8
NX = 4
HALF = NB // 2
BF = jnp.bfloat16
F32 = jnp.float32
VMEM = 48 * 1024 * 1024


def params():
    return pltpu.CompilerParams(vmem_limit_bytes=VMEM)


def shift(v, axis, step, n):
    return lax.ppermute(v, axis, [(i, (i + step) % n) for i in range(n)])


def flip(v, axis):
    return lax.ppermute(v, axis, [(0, 1), (1, 0)])


def ring(v, axis, n):
    out = {0: v}
    up = down = v
    half = v.shape[0] // 2
    for s in range(1, n // 2):
        up = shift(up, axis, 1, n)
        down = shift(down, axis, -1, n)
        out[n - s] = up
        out[s] = down
    a = shift(up[:half], axis, 1, n)
    b = shift(down[half:], axis, -1, n)
    out[n // 2] = jnp.concatenate([a, b], axis=0)
    return jnp.stack([out[j] for j in range(n)])


def onehot_pick(table, index):
    hit = index[:, None] == jnp.arange(table.shape[0], dtype=jnp.int32)[None, :]
    return jnp.sum(jnp.where(hit, table[None, :], 0), axis=1).astype(jnp.int32)


def block_maps(child_row, merged_row):
    target = jnp.arange(NB, dtype=jnp.int32)
    hits = merged_row[None, :] == target[:, None]
    filled = jnp.any(hits, axis=1)
    place = jnp.sum(jnp.where(hits, jnp.arange(merged_row.shape[0], dtype=jnp.int32)[None, :] + 4, 0), axis=1)
    before = target[None, :] < target[:, None]
    rank = jnp.sum(jnp.where(before & ~filled[None, :], 1, 0), axis=1)
    first_index = jnp.where(filled, place, rank).astype(jnp.int32)
    child_hits = child_row[None, :] == first_index[:, None]
    source = jnp.sum(jnp.where(child_hits, target[None, :], 0), axis=1).astype(jnp.int32)
    wanted = jnp.arange(4, dtype=jnp.int32)
    pivot = (~filled)[None, :] & (rank[None, :] == wanted[:, None])
    pivot_places = jnp.sum(jnp.where(pivot, target[None, :], 0), axis=1).astype(jnp.int32)
    return source, filled.astype(jnp.int32), pivot_places


def panel_blocks(rows, source, ok, core):
    def body(src, okr, ce, a, keep, send):
        s = pl.program_id(0)
        e = ce[0]
        for out, r in ((keep, e), (send, 1 - e)):
            part = a[0, pl.ds(pl.multiple_of(r * BLOCK, BLOCK), BLOCK), :]
            out[...] = jnp.where(okr[s * 2 + r] > 0, part, jnp.zeros_like(part))
    one = jax.ShapeDtypeStruct((BLOCK, 8 * BLOCK), BF)
    return pl.pallas_call(
        body,
        out_shape=(one, one),
        grid_spec=pltpu.PrefetchScalarGridSpec(
            num_scalar_prefetch=3,
            grid=(8,),
            in_specs=[pl.BlockSpec((1, 2 * BLOCK, BLOCK), lambda i, s, o, c: (s[i] // 2, 0, s[i] % 2))],
            out_specs=[pl.BlockSpec((BLOCK, BLOCK), lambda i, s, o, c: (0, i))] * 2,
        ),
        compiler_params=params(),
    )(source, ok, core, rows)


def few_blocks(rows, source):
    few = rows.shape[1]

    def body(src, *refs):
        for i in range(6):
            refs[-1][:, i * BLOCK:(i + 1) * BLOCK] = refs[i][0]

    def where_from(i):
        return lambda g, s: (s[i] // 2, 0, s[i] % 2)
    return pl.pallas_call(
        body,
        out_shape=jax.ShapeDtypeStruct((few, 6 * BLOCK), BF),
        grid_spec=pltpu.PrefetchScalarGridSpec(
            num_scalar_prefetch=1,
            grid=(1,),
            in_specs=[pl.BlockSpec((1, few, BLOCK), where_from(i)) for i in range(6)],
            out_specs=pl.BlockSpec((few, 6 * BLOCK), lambda g, s: (0, 0)),
        ),
        compiler_params=params(),
    )(source, *[rows] * 6)


def tile_parts(rows, source, ok):
    def body(src, okr, *refs):
        k, x = pl.program_id(0), pl.program_id(1)
        o = refs[-1]
        for z in range(NZ):
            c = 2 * (z * NX + x) + k
            for r in range(2):
                part = refs[z][0, r * BLOCK:(r + 1) * BLOCK, :]
                o[r, 0, 0, z] = jnp.where(okr[c * 2 + r] > 0, part, jnp.zeros_like(part))

    def where_from(z):
        def index(k, x, s, o):
            b = s[2 * (z * NX + x) + k]
            return (b // 2, 0, b % 2)
        return index
    return pl.pallas_call(
        body,
        out_shape=jax.ShapeDtypeStruct((2, 2, NX, NZ, BLOCK, BLOCK), BF),
        grid_spec=pltpu.PrefetchScalarGridSpec(
            num_scalar_prefetch=2,
            grid=(2, NX),
            in_specs=[pl.BlockSpec((1, 2 * BLOCK, BLOCK), where_from(z)) for z in range(NZ)],
            out_specs=pl.BlockSpec((2, 1, 1, NZ, BLOCK, BLOCK), lambda k, x, s, o: (0, k, x, 0, 0, 0)),
        ),
        compiler_params=params(),
    )(source, ok, *[rows] * NZ)


def mm(a, b):
    return jnp.dot(a, b, preferred_element_type=F32)


def mm_t(a, b):
    return lax.dot_general(a, b, (((1,), (1,)), ((), ())), preferred_element_type=F32)


def factor_rows(mine, other, special, w_one, w_two, yp):
    n = PANEL

    def body(y, a_ref, b_ref, s_ref, w1, w2, c_out, l_out):
        low = y[0] == 0
        a, b = a_ref[...], b_ref[...]
        both = (jnp.where(low, a, b), jnp.where(low, b, a))
        panel = (a[:, 2 * n:].astype(F32) + b[:, 2 * n:].astype(F32)).astype(BF).astype(F32)
        lead = s_ref[2 * n:, 4 * n:].astype(F32)
        for p in range(2):
            piv = s_ref[:n, 2 * p * n:(2 * p + 1) * n]
            t0 = s_ref[n:, 2 * p * n:(2 * p + 1) * n]
            t1 = s_ref[n:, (2 * p + 1) * n:(2 * p + 2) * n].astype(F32)
            tl0 = mm(t0, w1[p, 0]).astype(BF)
            tc1 = (t1 - mm_t(tl0, piv)).astype(BF)
            tl1 = mm(tc1[n:], w1[p, 1]).astype(BF)
            lead = lead - mm_t(tl0[n:], t0[:n]) - mm_t(tl1, tc1[:n])
            c0 = both[p][:, :n]
            l0 = mm(c0, w1[p, 0]).astype(BF)
            c1 = (both[p][:, n:2 * n].astype(F32) - mm_t(l0, piv)).astype(BF)
            l1 = mm(c1, w1[p, 1]).astype(BF)
            panel = panel - mm_t(l0, t0) - mm_t(l1, tc1)
            c_out[:, 2 * p * n:(2 * p + 1) * n] = c0
            c_out[:, (2 * p + 1) * n:(2 * p + 2) * n] = c1
            l_out[:, 2 * p * n:(2 * p + 1) * n] = l0
            l_out[:, (2 * p + 1) * n:(2 * p + 2) * n] = l1
        d0 = panel[:, :n].astype(BF)
        k0 = mm(d0, w2[0]).astype(BF)
        d1 = (panel[:, n:] - mm_t(k0, lead.astype(BF))).astype(BF)
        k1 = mm(d1, w2[1]).astype(BF)
        c_out[:, 4 * n:5 * n] = d0
        c_out[:, 5 * n:] = d1
        l_out[:, 4 * n:5 * n] = k0
        l_out[:, 5 * n:] = k1

    out = jax.ShapeDtypeStruct((BLOCK, 6 * n), BF)
    vm = pl.BlockSpec(memory_space=pltpu.VMEM)
    return pl.pallas_call(
        body,
        out_shape=(out, out),
        in_specs=[pl.BlockSpec(memory_space=pltpu.SMEM)] + [vm] * 5,
        out_specs=(vm, vm),
        compiler_params=params(),
    )(yp, mine, other, special, w_one, w_two)


def tile_update(parts, lower, columns, place):
    depth = lower.shape[-1]
    half = BLOCK // 2

    def body(zs, parts_ref, l_ref, c_ref, o_ref):
        c = c_ref[0]
        for x in range(NX):
            total = None
            for pair in range(2):
                s = (parts_ref[2 * pair, x, 0].astype(F32) + parts_ref[2 * pair + 1, x, 0].astype(F32)).astype(BF).astype(F32)
                total = s if total is None else total + s
            done = (total - mm_t(l_ref[(x + NX - zs[1]) % NX], c)).astype(BF)
            o_ref[x, 0] = done[:half]
            o_ref[NX + x, 0] = done[half:]

    return pl.pallas_call(
        body,
        out_shape=jax.ShapeDtypeStruct((2 * NX, NZ, half, BLOCK), BF),
        grid_spec=pltpu.PrefetchScalarGridSpec(
            num_scalar_prefetch=1,
            grid=(NZ,),
            in_specs=[
                pl.BlockSpec((4, NX, 1, BLOCK, BLOCK), lambda j, s: (0, 0, (s[0] + j) % NZ, 0, 0)),
                pl.BlockSpec((NX, BLOCK, depth), lambda j, s: (0, 0, 0)),
                pl.BlockSpec((1, BLOCK, depth), lambda j, s: (j, 0, 0)),
            ],
            out_specs=pl.BlockSpec((2 * NX, 1, half, BLOCK), lambda j, s: (0, (s[0] + j) % NZ, 0, 0)),
        ),
        compiler_params=params(),
    )(place, parts, lower, columns)


def join_rows(pieces):
    half = BLOCK // 2

    def body(a, o):
        for k in range(2):
            for x in range(NX):
                c = 2 * x + k
                o[:, c * BLOCK:(c + 1) * BLOCK] = a[k * NX + x, 0]
    return pl.pallas_call(
        body,
        out_shape=jax.ShapeDtypeStruct((half, NB * BLOCK), BF),
        grid=(NZ,),
        in_specs=[pl.BlockSpec((2 * NX, 1, half, BLOCK), lambda z: (0, z, 0, 0))],
        out_specs=pl.BlockSpec((half, 2 * NX * BLOCK), lambda z: (0, z)),
        compiler_params=params(),
    )(pieces)


def local(child_blocks, child_map, merged_map, pivots_one, pivots_two):
    q, yp, e = lax.axis_index("q"), lax.axis_index("yp"), lax.axis_index("core")
    z, x = lax.axis_index("z"), lax.axis_index("x")
    child = (q * 2 + yp) * 2 + e
    spot = z * NX + x
    slab = child_blocks[0].reshape(NB, BLOCK, 2 * BLOCK)
    source, filled, pivot_places = block_maps(child_map[child], merged_map[child // 2])

    own_filled = lax.dynamic_slice_in_dim(filled, 2 * spot, 2)
    lead_filled = filled[:4]
    panel_src = onehot_pick(source, jnp.concatenate([pivot_places, jnp.arange(4, dtype=jnp.int32)]))
    col_ok = jnp.concatenate([jnp.ones((4,), jnp.int32), lead_filled])

    row_src = onehot_pick(source, jnp.concatenate([pivot_places[2:], jnp.arange(4, dtype=jnp.int32)]))
    few = 6 * BLOCK // (NZ * NX)
    first = jnp.take(slab, row_src, axis=0).reshape(NZ * NX, few, 2 * BLOCK)
    first = lax.all_to_all(first, ("z", "x"), split_axis=0, concat_axis=0, tiled=True)
    part_of = (spot * few + jnp.arange(few, dtype=jnp.int32)) // BLOCK
    row_ok = onehot_pick(jnp.concatenate([jnp.ones((2,), jnp.int32), lead_filled]), part_of)
    first = few_blocks(first, panel_src)
    first_ok = (row_ok[:, None] * jnp.repeat(col_ok, BLOCK)[None, :6 * BLOCK]) > 0
    first = jnp.where(first_ok, first, jnp.zeros_like(first))
    first = (first.astype(F32) + flip(first, "core").astype(F32)).astype(BF)
    second = flip(first, "yp")
    low = jnp.where(yp == 0, first, second)
    high = jnp.where(yp == 0, second, first)
    lead = (low[:, 2 * PANEL:].astype(F32) + high[:, 2 * PANEL:].astype(F32)).astype(BF)
    special = jnp.concatenate([low[:, :2 * PANEL], high[:, :2 * PANEL], lead], axis=1)
    special = lax.all_gather(special, ("z", "x"), axis=0, tiled=True)

    sent = jnp.take(slab, source, axis=0).reshape(NZ * NX, 2 * BLOCK, 2 * BLOCK)
    rows = lax.all_to_all(sent, ("z", "x"), split_axis=0, concat_axis=0, tiled=True)

    panel_ok = (col_ok[:, None] * own_filled[None, :]).reshape(-1)
    keep, send = panel_blocks(rows, panel_src, panel_ok, e.reshape(1))
    got = flip(send, "core")
    mine = (keep.astype(F32) + got.astype(F32)).astype(BF)
    other = flip(mine, "yp")
    w_one = lax.dynamic_slice_in_dim(pivots_one, 2 * q, 2)
    w_two = lax.dynamic_index_in_dim(pivots_two, q, keepdims=False)
    columns, lower = factor_rows(mine, other, special, w_one, w_two, yp.reshape(1))

    tile_ok = (filled[:, None] * own_filled[None, :]).reshape(-1)
    parts = tile_parts(rows, source, tile_ok)
    parts = lax.all_to_all(parts.reshape(4 * NX, NZ, BLOCK, BLOCK), ("yp", "core", "x"), split_axis=0, concat_axis=0, tiled=True)

    columns = ring(columns, "z", NZ)
    swapped = flip(lower, "core")
    lower = ring(jnp.where(e == yp, lower, swapped), "x", NX)

    done = tile_update(parts.reshape(4, NX, NZ, BLOCK, BLOCK), lower, columns, jnp.stack([z, x]))
    done = lax.all_to_all(done, ("core", "x"), split_axis=0, concat_axis=0, tiled=True)
    return join_rows(done)[None, None]


def solution(mesh):
    fine = Mesh(mesh.devices.reshape(2, 2, 2, NZ, NX), ("q", "yp", "core", "z", "x"))
    leaf, plane = ("q", "yp", "core"), ("z", "x")
    return jax.shard_map(
        local,
        mesh=fine,
        in_specs=(P(leaf, None, plane), P(), P(), P(), P()),
        out_specs=P(plane, leaf, None, None),
        check_vma=False,
    )
```

```python
import jax
import jax.numpy as jnp
from jax import lax
from jax.experimental import pallas as pl
from jax.experimental.pallas import tpu as pltpu
from jax.sharding import Mesh, PartitionSpec as P

BLOCK = 128
PANEL = 256
NB = 64
NZ = 8
NX = 4
HALF = NB // 2
BF = jnp.bfloat16
F32 = jnp.float32
VMEM = 24 * 1024 * 1024
LARGE = 56 * 1024 * 1024


def params(limit=VMEM):
    return pltpu.CompilerParams(vmem_limit_bytes=limit)


def cost(us):
    return pl.CostEstimate(flops=0, bytes_accessed=int(us * 3.6e5), transcendentals=0)


def shift(v, axis, step, n):
    return lax.ppermute(v, axis, [(i, (i + step) % n) for i in range(n)])


def flip(v, axis):
    return lax.ppermute(v, axis, [(0, 1), (1, 0)])


ANY = pl.BlockSpec(memory_space=pl.ANY)


def tie(values, *earlier):
    n = len(values)
    return pl.pallas_call(
        lambda *refs: None,
        out_shape=tuple(jax.ShapeDtypeStruct(v.shape, v.dtype) for v in values),
        in_specs=[ANY] * (n + len(earlier)),
        out_specs=(ANY,) * n,
        cost_estimate=cost(0.5),
        input_output_aliases={i: i for i in range(n)},
    )(*values, *earlier)


def both_ways(pair, axis, n):
    return shift(pair[0], axis, 1, n), shift(pair[1], axis, -1, n)


def onehot_pick(table, index):
    hit = index[:, None] == jnp.arange(table.shape[0], dtype=jnp.int32)[None, :]
    return jnp.sum(jnp.where(hit, table[None, :], 0), axis=1).astype(jnp.int32)


def block_maps(child_row, merged_row):
    target = jnp.arange(NB, dtype=jnp.int32)
    hits = merged_row[None, :] == target[:, None]
    filled = jnp.any(hits, axis=1)
    place = jnp.sum(jnp.where(hits, jnp.arange(merged_row.shape[0], dtype=jnp.int32)[None, :] + 4, 0), axis=1)
    before = target[None, :] < target[:, None]
    rank = jnp.sum(jnp.where(before & ~filled[None, :], 1, 0), axis=1)
    first_index = jnp.where(filled, place, rank).astype(jnp.int32)
    child_hits = child_row[None, :] == first_index[:, None]
    source = jnp.sum(jnp.where(child_hits, target[None, :], 0), axis=1).astype(jnp.int32)
    wanted = jnp.arange(4, dtype=jnp.int32)
    pivot = (~filled)[None, :] & (rank[None, :] == wanted[:, None])
    pivot_places = jnp.sum(jnp.where(pivot, target[None, :], 0), axis=1).astype(jnp.int32)
    return source, filled.astype(jnp.int32), pivot_places


def panel_blocks(rows, source, ok, core, *earlier):
    def body(src, okr, ce, *refs):
        e = ce[0]
        for i in range(8):
            for out, r in ((refs[-2], e), (refs[-1], 1 - e)):
                part = refs[i][0, pl.ds(pl.multiple_of(r * BLOCK, BLOCK), BLOCK), :]
                out[:, i * BLOCK:(i + 1) * BLOCK] = jnp.where(okr[i * 2 + r] > 0, part, jnp.zeros_like(part))

    def where_from(i):
        return lambda g, s, o, c: (s[i] // 2, 0, s[i] % 2)
    one = jax.ShapeDtypeStruct((BLOCK, 8 * BLOCK), BF)
    return pl.pallas_call(
        body,
        out_shape=(one, one),
        grid_spec=pltpu.PrefetchScalarGridSpec(
            num_scalar_prefetch=3,
            grid=(1,),
            in_specs=[pl.BlockSpec((1, 2 * BLOCK, BLOCK), where_from(i)) for i in range(8)] + [ANY] * len(earlier),
            out_specs=[pl.BlockSpec((BLOCK, 8 * BLOCK), lambda g, s, o, c: (0, 0))] * 2,
        ),
        cost_estimate=cost(1.8),
        compiler_params=params(),
    )(source, ok, core, *[rows] * 8, *earlier)


def core_send(rows, source, core, *earlier):
    def body(src, ce, rows_ref, *refs):
        far, held, sems, out_sems = refs[-4:]
        ins, outs = [], []
        for x in range(NX):
            for z in range(NZ):
                b = src[2 * (z * NX + x) + 1 - ce[0]]
                lanes = pl.ds(pl.multiple_of(b % 2 * BLOCK, BLOCK), BLOCK)
                ins.append(pltpu.make_async_copy(rows_ref.at[b // 2, :, lanes], held.at[x, z], sems.at[x, z]))
                ins[-1].start()
        for x in range(NX):
            for z in range(NZ):
                ins[x * NZ + z].wait()
            outs.append(pltpu.make_async_copy(held.at[x], far.at[x], out_sems.at[x]))
            outs[-1].start()
        for move in outs:
            move.wait()

    shape = (NX, NZ, 2 * BLOCK, BLOCK)
    return pl.pallas_call(
        body,
        out_shape=jax.ShapeDtypeStruct(shape, BF),
        grid_spec=pltpu.PrefetchScalarGridSpec(
            num_scalar_prefetch=2,
            grid=(1,),
            in_specs=[ANY] * (1 + len(earlier)),
            out_specs=ANY,
            scratch_shapes=[
                pltpu.VMEM(shape, BF),
                pltpu.SemaphoreType.DMA((NX, NZ)),
                pltpu.SemaphoreType.DMA((NX,)),
            ],
        ),
        cost_estimate=cost(3.3),
        compiler_params=params(),
    )(source, core, rows, *earlier)


def pick_rows(slab, source):
    n = source.shape[0]

    def body(src, *refs):
        for i in range(n):
            refs[-1][i] = refs[i][0]
    shape = (n,) + slab.shape[1:]

    def where_from(i):
        return lambda g, s: (s[i], 0, 0)
    return pl.pallas_call(
        body,
        out_shape=jax.ShapeDtypeStruct(shape, BF),
        grid_spec=pltpu.PrefetchScalarGridSpec(
            num_scalar_prefetch=1,
            grid=(1,),
            in_specs=[pl.BlockSpec((1,) + slab.shape[1:], where_from(i)) for i in range(n)],
            out_specs=pl.BlockSpec(shape, lambda g, s: (0, 0, 0)),
        ),
        cost_estimate=cost(1.3),
        compiler_params=params(),
    )(source, *[slab] * n)


def few_blocks(rows, source):
    few = rows.shape[1]

    def body(src, *refs):
        for i in range(6):
            refs[-1][:, i * BLOCK:(i + 1) * BLOCK] = refs[i][0]

    def where_from(i):
        return lambda g, s: (s[i] // 2, 0, s[i] % 2)
    return pl.pallas_call(
        body,
        out_shape=jax.ShapeDtypeStruct((few, 6 * BLOCK), BF),
        grid_spec=pltpu.PrefetchScalarGridSpec(
            num_scalar_prefetch=1,
            grid=(1,),
            in_specs=[pl.BlockSpec((1, few, BLOCK), where_from(i)) for i in range(6)],
            out_specs=pl.BlockSpec((few, 6 * BLOCK), lambda g, s: (0, 0)),
        ),
        cost_estimate=cost(0.6),
        compiler_params=params(),
    )(source, *[rows] * 6)


STEP = NZ


def column_specs(core_of):
    def where_from(i):
        def index(x, w, s, o, c):
            b = s[2 * ((w * STEP + i) * NX + x) + core_of(c[0])]
            return (b // 2, 0, b % 2)
        return index
    return [pl.BlockSpec((1, 2 * BLOCK, BLOCK), where_from(i)) for i in range(STEP)]


def core_sum(rows, got, source, ok, place):
    def body(src, okr, ce, *refs):
        x, w = pl.program_id(0), pl.program_id(1)
        keep, send = refs[-2:]
        for i in range(STEP):
            c = 2 * ((w * STEP + i) * NX + x) + ce[0]
            for out, r in ((keep, ce[1]), (send, 1 - ce[1])):
                part = pl.ds(pl.multiple_of(r * BLOCK, BLOCK), BLOCK)
                total = (refs[i][0, part, :].astype(F32) + refs[STEP][0, i, part, :].astype(F32)).astype(BF)
                out[0, i] = jnp.where(okr[c * 2 + r] > 0, total, jnp.zeros_like(total))

    one = jax.ShapeDtypeStruct((NX, NZ, BLOCK, BLOCK), BF)
    return pl.pallas_call(
        body,
        out_shape=(one, one),
        grid_spec=pltpu.PrefetchScalarGridSpec(
            num_scalar_prefetch=3,
            grid=(NX, NZ // STEP),
            in_specs=column_specs(lambda e: e) + [
                pl.BlockSpec((1, STEP, 2 * BLOCK, BLOCK), lambda x, w, s, o, c: (x, w, 0, 0))],
            out_specs=[pl.BlockSpec((1, STEP, BLOCK, BLOCK), lambda x, w, s, o, c: (x, w, 0, 0))] * 2,
        ),
        cost_estimate=cost(4.2),
        compiler_params=params(),
    )(source, ok, place, *[rows] * STEP, got)


def mm(a, b):
    return jnp.dot(a, b, preferred_element_type=F32)


def mm_t(a, b):
    return lax.dot_general(a, b, (((1,), (1,)), ((), ())), preferred_element_type=F32)


def lead_rows(special, w_one, place):
    n = PANEL

    def body(y, s_ref, w1, t_out, lead_out):
        lead = s_ref[2 * n:, 4 * n:].astype(F32)
        for p in range(2):
            low = slice(2 * p * n, (2 * p + 1) * n)
            high = slice((2 * p + 1) * n, (2 * p + 2) * n)
            t0 = s_ref[n:, low]
            l0 = mm(t0, w1[p, 0]).astype(BF)
            t1 = (s_ref[n:, high].astype(F32) - mm_t(l0, s_ref[:n, low])).astype(BF)
            l1 = mm(t1[n:], w1[p, 1]).astype(BF)
            lead = lead - mm_t(l0[n:], t0[:n]) - mm_t(l1, t1[:n])
            t_out[:, low] = t0
            t_out[:, high] = t1
        lead_out[...] = lead.astype(BF)

    def whole(v):
        return pl.BlockSpec(v.shape, lambda g, y: (0, 0))
    out = jax.ShapeDtypeStruct((2 * n, 4 * n), BF), jax.ShapeDtypeStruct((n, n), BF)
    return pl.pallas_call(
        body,
        out_shape=out,
        grid_spec=pltpu.PrefetchScalarGridSpec(
            num_scalar_prefetch=1,
            grid=(1,),
            in_specs=[whole(special), pl.BlockSpec((2, 2, n, n), lambda g, y: (y[1], 0, 0, 0))],
            out_specs=[whole(v) for v in out],
        ),
        cost_estimate=cost(1.6),
        compiler_params=params(),
    )(place, special, w_one)


def factor_rows(mine, other, special, lead, w_one, w_two, place, *earlier):
    n = PANEL

    def body(y, a_ref, b_ref, p0, p1, t_ref, lead_ref, w1, w2, *refs):
        c_out, l_out = refs[-2:]
        first = y[0] == 0
        a, b = a_ref[...], b_ref[...]
        both = (jnp.where(first, a, b), jnp.where(first, b, a))
        panel = (a[:, 2 * n:].astype(F32) + b[:, 2 * n:].astype(F32)).astype(BF).astype(F32)
        for p in range(2):
            low = slice(2 * p * n, (2 * p + 1) * n)
            high = slice((2 * p + 1) * n, (2 * p + 2) * n)
            c0 = both[p][:, :n]
            l0 = mm(c0, w1[p, 0]).astype(BF)
            c1 = (both[p][:, n:2 * n].astype(F32) - mm_t(l0, (p0, p1)[p][...])).astype(BF)
            l1 = mm(c1, w1[p, 1]).astype(BF)
            panel = panel - mm_t(l0, t_ref[:, low]) - mm_t(l1, t_ref[:, high])
            c_out[:, p * n:(p + 1) * n] = c1
            l_out[:, p * n:(p + 1) * n] = l0
            l_out[:, (2 + p) * n:(3 + p) * n] = l1
        d0 = panel[:, :n].astype(BF)
        k0 = mm(d0, w2[0, 0]).astype(BF)
        d1 = (panel[:, n:] - mm_t(k0, lead_ref[...])).astype(BF)
        c_out[:, 2 * n:3 * n] = d0
        c_out[:, 3 * n:] = d1
        l_out[:, 4 * n:5 * n] = k0
        l_out[:, 5 * n:] = mm(d1, w2[0, 1]).astype(BF)

    def whole(v):
        return pl.BlockSpec(v.shape, lambda g, y: (0, 0))
    out = [jax.ShapeDtypeStruct((BLOCK, k * n), BF) for k in (4, 6)]
    return pl.pallas_call(
        body,
        out_shape=out,
        grid_spec=pltpu.PrefetchScalarGridSpec(
            num_scalar_prefetch=1,
            grid=(1,),
            in_specs=[
                whole(mine), whole(other),
                pl.BlockSpec((n, n), lambda g, y: (0, 0)),
                pl.BlockSpec((n, n), lambda g, y: (0, 2)),
                whole(lead[0]), whole(lead[1]),
                pl.BlockSpec((2, 2, n, n), lambda g, y: (y[1], 0, 0, 0)),
                pl.BlockSpec((1, 2, n, n), lambda g, y: (y[1], 0, 0, 0)),
            ] + [ANY] * len(earlier),
            out_specs=[whole(v) for v in out],
        ),
        cost_estimate=cost(3.5),
        compiler_params=params(),
    )(place, mine, other, special, special, *lead, w_one, w_two, *earlier)


def tile_update(parts, lower, first, columns, place):
    half = BLOCK // 2
    deep = first.shape[-1]

    def body(zs, *refs):
        part, head, l_refs, c_refs = refs[:2], refs[2:4], refs[4:4 + NX], refs[4 + NX:4 + NX + NZ]
        out, low = refs[-2:]

        @pl.when(pl.program_id(0) == 0)
        def _():
            for i in range(NX):
                low[pl.ds(pl.multiple_of((zs[1] + i) % NX * BLOCK, BLOCK), BLOCK), :] = l_refs[i][...]

        for step in range(NZ // 2):
            @pl.when(pl.program_id(0) == step)
            def _():
                c = jnp.concatenate([c_refs[2 * step][...], c_refs[2 * step + 1][...]], axis=0)
                update = mm_t(low[:, deep:], c) + mm_t(low[:, :deep], jnp.concatenate([head[0][0], head[1][0]], axis=0))
                for j in range(2):
                    for x in range(NX):
                        rows = slice(x * BLOCK, (x + 1) * BLOCK)
                        done = (part[j][x, 0].astype(F32) - update[rows, j * BLOCK:(j + 1) * BLOCK]).astype(BF)
                        out[x, j] = done[:half]
                        out[NX + x, j] = done[half:]

    def part_spec(j):
        return pl.BlockSpec((NX, 1, BLOCK, BLOCK), lambda g, s: (0, (s[0] + 2 * g + j) % NZ, 0, 0))

    def head_spec(j):
        return pl.BlockSpec((1, BLOCK, deep), lambda g, s: ((s[0] + 2 * g + j) % NZ, 0, 0))

    def whole(v):
        return pl.BlockSpec(v.shape, lambda g, s: (0, 0))
    return pl.pallas_call(
        body,
        out_shape=jax.ShapeDtypeStruct((2 * NX, NZ, half, BLOCK), BF),
        grid_spec=pltpu.PrefetchScalarGridSpec(
            num_scalar_prefetch=1,
            grid=(NZ // 2,),
            in_specs=[part_spec(0), part_spec(1), head_spec(0), head_spec(1)] + [whole(v) for v in (*lower, *columns)],
            out_specs=pl.BlockSpec((2 * NX, 2, half, BLOCK), lambda g, s: (0, g, 0, 0)),
            scratch_shapes=[pltpu.VMEM((NX * BLOCK, lower[0].shape[1]), BF)],
        ),
        cost_estimate=cost(7),
        compiler_params=params(LARGE),
    )(place, parts, parts, first, first, *lower, *columns)


def join_rows(pieces, place):
    half = BLOCK // 2
    wide = 2 * NX * BLOCK
    some = NZ // 2

    def body(zs, *refs):
        for i in range(some):
            for k in range(2):
                for x in range(NX):
                    c = i * wide + (2 * x + k) * BLOCK
                    refs[-1][:, c:c + BLOCK] = refs[i][k * NX + x, 0]

    def where_from(i):
        return lambda g, s: (0, (g * some + i + NZ - s[0]) % NZ, 0, 0)
    return pl.pallas_call(
        body,
        out_shape=jax.ShapeDtypeStruct((half, NB * BLOCK), BF),
        grid_spec=pltpu.PrefetchScalarGridSpec(
            num_scalar_prefetch=1,
            grid=(NZ // some,),
            in_specs=[pl.BlockSpec((2 * NX, 1, half, BLOCK), where_from(i)) for i in range(some)],
            out_specs=pl.BlockSpec((half, some * wide), lambda g, s: (0, g)),
        ),
        cost_estimate=cost(2.2),
        compiler_params=params(),
    )(place, *[pieces] * some)


def local(child_blocks, child_map, merged_map, pivots_one, pivots_two):
    q, yp, e = lax.axis_index("q"), lax.axis_index("yp"), lax.axis_index("core")
    z, x = lax.axis_index("z"), lax.axis_index("x")
    child = (q * 2 + yp) * 2 + e
    spot = z * NX + x
    slab = child_blocks[0].reshape(NB, BLOCK, 2 * BLOCK)
    source, filled, pivot_places = block_maps(child_map[child], merged_map[child // 2])

    own_filled = lax.dynamic_slice_in_dim(filled, 2 * spot, 2)
    lead_filled = filled[:4]
    panel_src = onehot_pick(source, jnp.concatenate([pivot_places, jnp.arange(4, dtype=jnp.int32)]))
    col_ok = jnp.concatenate([jnp.ones((4,), jnp.int32), lead_filled])

    row_src = onehot_pick(source, jnp.concatenate([pivot_places[2:], jnp.arange(4, dtype=jnp.int32)]))
    few = 6 * BLOCK // (NZ * NX)
    first = pick_rows(slab, row_src).reshape(NZ * NX, few, 2 * BLOCK)
    first = lax.all_to_all(first, ("z", "x"), split_axis=0, concat_axis=0, tiled=True)
    part_of = (spot * few + jnp.arange(few, dtype=jnp.int32)) // BLOCK
    row_ok = onehot_pick(jnp.concatenate([jnp.ones((2,), jnp.int32), lead_filled]), part_of)
    first = few_blocks(first, panel_src)
    first_ok = (row_ok[:, None] * jnp.repeat(col_ok, BLOCK)[None, :6 * BLOCK]) > 0
    first = jnp.where(first_ok, first, jnp.zeros_like(first))
    first = (first.astype(F32) + flip(first, "core").astype(F32)).astype(BF)
    second = flip(first, "yp")
    low = jnp.where(yp == 0, first, second)
    high = jnp.where(yp == 0, second, first)
    lead = (low[:, 2 * PANEL:].astype(F32) + high[:, 2 * PANEL:].astype(F32)).astype(BF)
    special = jnp.concatenate([low[:, :2 * PANEL], high[:, :2 * PANEL], lead], axis=1)
    special = lax.all_gather(special, ("z", "x"), axis=0, tiled=True)

    sent = slab.at[source].get(mode="promise_in_bounds").reshape(NZ * NX, 2 * BLOCK, 2 * BLOCK)
    rows = lax.all_to_all(sent, ("z", "x"), split_axis=0, concat_axis=0, tiled=True)

    panel_ok = (col_ok[:, None] * own_filled[None, :]).reshape(-1)
    core = e.reshape(1)
    tile_ok = (filled[:, None] * own_filled[None, :]).reshape(-1)
    group = jnp.stack([yp, q])
    lead = lead_rows(special, pivots_one, group)
    keep, send = panel_blocks(rows, panel_src, panel_ok, core, *lead)
    mine = (keep.astype(F32) + flip(send, "core").astype(F32)).astype(BF)
    other = flip(mine, "yp")
    tile_got = flip(core_send(rows, source, core, mine), "core")
    first = jnp.concatenate([
        jnp.where(yp == 0, mine, other)[:, :PANEL], jnp.where(yp == 0, other, mine)[:, :PANEL]], axis=1)
    first = lax.all_gather(first, "z", axis=0, tiled=False)
    own, theirs = core_sum(rows, tile_got, source, tile_ok, jnp.stack([e, yp]))
    columns, lower = factor_rows(mine, other, special, lead, pivots_one, pivots_two, group, own)

    place = jnp.stack([z, x])
    z1 = tie(both_ways((columns, columns), "z", NZ))
    mate = flip(lower, "core")
    lower = jnp.where(e == yp, lower, mate)
    x1 = tie(both_ways((lower, lower), "x", NX))
    parts = (own.astype(F32) + flip(theirs, "yp").astype(F32)).astype(BF)
    x2 = shift(x1[0], "x", 1, NX)
    parts, = tie((parts,), x2)
    parts = lax.all_to_all(parts, "x", split_axis=0, concat_axis=0, tiled=True)
    z2 = tie(both_ways(z1, "z", NZ))
    z3 = tie(both_ways(z2, "z", NZ))
    z4 = shift(z3[0], "z", 1, NZ)
    lower = (lower, x1[1], x2, x1[0])

    columns = (columns, z1[1], z2[1], z3[1], z4, z3[0], z2[0], z1[0])
    done = tile_update(parts, lower, first, columns, place)
    done = lax.all_to_all(done, ("core", "x"), split_axis=0, concat_axis=0, tiled=True)
    return join_rows(done, place)[None, None]


def solution(mesh):
    fine = Mesh(mesh.devices.reshape(2, 2, 2, NZ, NX), ("q", "yp", "core", "z", "x"))
    leaf, plane = ("q", "yp", "core"), ("z", "x")
    return jax.shard_map(
        local,
        mesh=fine,
        in_specs=(P(leaf, None, plane), P(), P(), P(), P()),
        out_specs=P(plane, leaf, None, None),
        check_vma=False,
    )
```

```python
import jax
import jax.numpy as jnp
from jax import lax
from jax.experimental import pallas as pl
from jax.experimental.pallas import tpu as pltpu
from jax.sharding import Mesh, PartitionSpec as P

BLOCK = 128
PANEL = 256
NB = 64
NZ = 8
NX = 4
HALF = NB // 2
BF = jnp.bfloat16
F32 = jnp.float32
VMEM = 24 * 1024 * 1024
LARGE = 56 * 1024 * 1024


def params(limit=VMEM):
    return pltpu.CompilerParams(vmem_limit_bytes=limit)


def cost(us):
    return pl.CostEstimate(flops=0, bytes_accessed=int(us * 3.6e5), transcendentals=0)


def shift(v, axis, step, n):
    return lax.ppermute(v, axis, [(i, (i + step) % n) for i in range(n)])


def flip(v, axis):
    return lax.ppermute(v, axis, [(0, 1), (1, 0)])


ANY = pl.BlockSpec(memory_space=pl.ANY)


def tie(values, *earlier):
    n = len(values)
    return pl.pallas_call(
        lambda *refs: None,
        out_shape=tuple(jax.ShapeDtypeStruct(v.shape, v.dtype) for v in values),
        in_specs=[ANY] * (n + len(earlier)),
        out_specs=(ANY,) * n,
        cost_estimate=cost(0.5),
        input_output_aliases={i: i for i in range(n)},
    )(*values, *earlier)


def both_ways(pair, axis, n):
    return shift(pair[0], axis, 1, n), shift(pair[1], axis, -1, n)


def onehot_pick(table, index):
    hit = index[:, None] == jnp.arange(table.shape[0], dtype=jnp.int32)[None, :]
    return jnp.sum(jnp.where(hit, table[None, :], 0), axis=1).astype(jnp.int32)


def block_maps(child_row, merged_row):
    target = jnp.arange(NB, dtype=jnp.int32)
    hits = merged_row[None, :] == target[:, None]
    filled = jnp.any(hits, axis=1)
    place = jnp.sum(jnp.where(hits, jnp.arange(merged_row.shape[0], dtype=jnp.int32)[None, :] + 4, 0), axis=1)
    before = target[None, :] < target[:, None]
    rank = jnp.sum(jnp.where(before & ~filled[None, :], 1, 0), axis=1)
    first_index = jnp.where(filled, place, rank).astype(jnp.int32)
    child_hits = child_row[None, :] == first_index[:, None]
    source = jnp.sum(jnp.where(child_hits, target[None, :], 0), axis=1).astype(jnp.int32)
    wanted = jnp.arange(4, dtype=jnp.int32)
    pivot = (~filled)[None, :] & (rank[None, :] == wanted[:, None])
    pivot_places = jnp.sum(jnp.where(pivot, target[None, :], 0), axis=1).astype(jnp.int32)
    return source, filled.astype(jnp.int32), pivot_places


def panel_blocks(rows, source, ok, core, *earlier):
    def body(src, okr, ce, *refs):
        e = ce[0]
        for i in range(8):
            for out, r in ((refs[-2], e), (refs[-1], 1 - e)):
                part = refs[i][0, pl.ds(pl.multiple_of(r * BLOCK, BLOCK), BLOCK), :]
                out[:, i * BLOCK:(i + 1) * BLOCK] = jnp.where(okr[i * 2 + r] > 0, part, jnp.zeros_like(part))

    def where_from(i):
        return lambda g, s, o, c: (s[i] // 2, 0, s[i] % 2)
    one = jax.ShapeDtypeStruct((BLOCK, 8 * BLOCK), BF)
    return pl.pallas_call(
        body,
        out_shape=(one, one),
        grid_spec=pltpu.PrefetchScalarGridSpec(
            num_scalar_prefetch=3,
            grid=(1,),
            in_specs=[pl.BlockSpec((1, 2 * BLOCK, BLOCK), where_from(i)) for i in range(8)] + [ANY] * len(earlier),
            out_specs=[pl.BlockSpec((BLOCK, 8 * BLOCK), lambda g, s, o, c: (0, 0))] * 2,
        ),
        cost_estimate=cost(1.8),
        compiler_params=params(),
    )(source, ok, core, *[rows] * 8, *earlier)


def core_send(rows, source, core, *earlier):
    def body(src, ce, rows_ref, *refs):
        far, held, sems, out_sems = refs[-4:]
        ins, outs = [], []
        for x in range(NX):
            for z in range(NZ):
                b = src[2 * (z * NX + x) + 1 - ce[0]]
                lanes = pl.ds(pl.multiple_of(b % 2 * BLOCK, BLOCK), BLOCK)
                ins.append(pltpu.make_async_copy(rows_ref.at[b // 2, :, lanes], held.at[x, z], sems.at[x, z]))
                ins[-1].start()
        for x in range(NX):
            for z in range(NZ):
                ins[x * NZ + z].wait()
            outs.append(pltpu.make_async_copy(held.at[x], far.at[x], out_sems.at[x]))
            outs[-1].start()
        for move in outs:
            move.wait()

    shape = (NX, NZ, 2 * BLOCK, BLOCK)
    return pl.pallas_call(
        body,
        out_shape=jax.ShapeDtypeStruct(shape, BF),
        grid_spec=pltpu.PrefetchScalarGridSpec(
            num_scalar_prefetch=2,
            grid=(1,),
            in_specs=[ANY] * (1 + len(earlier)),
            out_specs=ANY,
            scratch_shapes=[
                pltpu.VMEM(shape, BF),
                pltpu.SemaphoreType.DMA((NX, NZ)),
                pltpu.SemaphoreType.DMA((NX,)),
            ],
        ),
        cost_estimate=cost(3.3),
        compiler_params=params(),
    )(source, core, rows, *earlier)


def pick_rows(slab, source):
    n = source.shape[0]

    def body(src, *refs):
        for i in range(n):
            refs[-1][i] = refs[i][0]
    shape = (n,) + slab.shape[1:]

    def where_from(i):
        return lambda g, s: (s[i], 0, 0)
    return pl.pallas_call(
        body,
        out_shape=jax.ShapeDtypeStruct(shape, BF),
        grid_spec=pltpu.PrefetchScalarGridSpec(
            num_scalar_prefetch=1,
            grid=(1,),
            in_specs=[pl.BlockSpec((1,) + slab.shape[1:], where_from(i)) for i in range(n)],
            out_specs=pl.BlockSpec(shape, lambda g, s: (0, 0, 0)),
        ),
        cost_estimate=cost(1.3),
        compiler_params=params(LARGE),
    )(source, *[slab] * n)


def few_blocks(rows, source):
    few = rows.shape[1]

    def body(src, *refs):
        for i in range(6):
            refs[-1][:, i * BLOCK:(i + 1) * BLOCK] = refs[i][0]

    def where_from(i):
        return lambda g, s: (s[i] // 2, 0, s[i] % 2)
    return pl.pallas_call(
        body,
        out_shape=jax.ShapeDtypeStruct((few, 6 * BLOCK), BF),
        grid_spec=pltpu.PrefetchScalarGridSpec(
            num_scalar_prefetch=1,
            grid=(1,),
            in_specs=[pl.BlockSpec((1, few, BLOCK), where_from(i)) for i in range(6)],
            out_specs=pl.BlockSpec((few, 6 * BLOCK), lambda g, s: (0, 0)),
        ),
        cost_estimate=cost(0.6),
        compiler_params=params(),
    )(source, *[rows] * 6)


STEP = NZ


def column_specs(core_of):
    def where_from(i):
        def index(x, w, s, o, c):
            b = s[2 * ((w * STEP + i) * NX + x) + core_of(c[0])]
            return (b // 2, 0, b % 2)
        return index
    return [pl.BlockSpec((1, 2 * BLOCK, BLOCK), where_from(i)) for i in range(STEP)]


def core_sum(rows, got, source, ok, place):
    def body(src, okr, ce, *refs):
        x, w = pl.program_id(0), pl.program_id(1)
        keep, send = refs[-2:]
        for i in range(STEP):
            c = 2 * ((w * STEP + i) * NX + x) + ce[0]
            for out, r in ((keep, ce[1]), (send, 1 - ce[1])):
                part = pl.ds(pl.multiple_of(r * BLOCK, BLOCK), BLOCK)
                total = (refs[i][0, part, :].astype(F32) + refs[STEP][0, i, part, :].astype(F32)).astype(BF)
                out[0, i] = jnp.where(okr[c * 2 + r] > 0, total, jnp.zeros_like(total))

    one = jax.ShapeDtypeStruct((NX, NZ, BLOCK, BLOCK), BF)
    return pl.pallas_call(
        body,
        out_shape=(one, one),
        grid_spec=pltpu.PrefetchScalarGridSpec(
            num_scalar_prefetch=3,
            grid=(NX, NZ // STEP),
            in_specs=column_specs(lambda e: e) + [
                pl.BlockSpec((1, STEP, 2 * BLOCK, BLOCK), lambda x, w, s, o, c: (x, w, 0, 0))],
            out_specs=[pl.BlockSpec((1, STEP, BLOCK, BLOCK), lambda x, w, s, o, c: (x, w, 0, 0))] * 2,
        ),
        cost_estimate=cost(4.2),
        compiler_params=params(),
    )(source, ok, place, *[rows] * STEP, got)


def mm(a, b):
    return jnp.dot(a, b, preferred_element_type=F32)


def mm_t(a, b):
    return lax.dot_general(a, b, (((1,), (1,)), ((), ())), preferred_element_type=F32)


def lead_rows(special, w_one, place):
    n = PANEL

    def body(y, s_ref, w1, t_out, lead_out):
        lead = s_ref[2 * n:, 4 * n:].astype(F32)
        for p in range(2):
            low = slice(2 * p * n, (2 * p + 1) * n)
            high = slice((2 * p + 1) * n, (2 * p + 2) * n)
            t0 = s_ref[n:, low]
            l0 = mm(t0, w1[p, 0]).astype(BF)
            t1 = (s_ref[n:, high].astype(F32) - mm_t(l0, s_ref[:n, low])).astype(BF)
            l1 = mm(t1[n:], w1[p, 1]).astype(BF)
            lead = lead - mm_t(l0[n:], t0[:n]) - mm_t(l1, t1[:n])
            t_out[:, low] = t0
            t_out[:, high] = t1
        lead_out[...] = lead.astype(BF)

    def whole(v):
        return pl.BlockSpec(v.shape, lambda g, y: (0, 0))
    out = jax.ShapeDtypeStruct((2 * n, 4 * n), BF), jax.ShapeDtypeStruct((n, n), BF)
    return pl.pallas_call(
        body,
        out_shape=out,
        grid_spec=pltpu.PrefetchScalarGridSpec(
            num_scalar_prefetch=1,
            grid=(1,),
            in_specs=[whole(special), pl.BlockSpec((2, 2, n, n), lambda g, y: (y[1], 0, 0, 0))],
            out_specs=[whole(v) for v in out],
        ),
        cost_estimate=cost(1.6),
        compiler_params=params(),
    )(place, special, w_one)


def factor_rows(mine, other, special, lead, w_one, w_two, place, *earlier):
    n = PANEL

    def body(y, a_ref, b_ref, p0, p1, t_ref, lead_ref, w1, w2, *refs):
        c_out, l_out = refs[-2:]
        first = y[0] == 0
        a, b = a_ref[...], b_ref[...]
        both = (jnp.where(first, a, b), jnp.where(first, b, a))
        panel = (a[:, 2 * n:].astype(F32) + b[:, 2 * n:].astype(F32)).astype(BF).astype(F32)
        for p in range(2):
            low = slice(2 * p * n, (2 * p + 1) * n)
            high = slice((2 * p + 1) * n, (2 * p + 2) * n)
            c0 = both[p][:, :n]
            l0 = mm(c0, w1[p, 0]).astype(BF)
            c1 = (both[p][:, n:2 * n].astype(F32) - mm_t(l0, (p0, p1)[p][...])).astype(BF)
            l1 = mm(c1, w1[p, 1]).astype(BF)
            panel = panel - mm_t(l0, t_ref[:, low]) - mm_t(l1, t_ref[:, high])
            c_out[:, p * n:(p + 1) * n] = c1
            l_out[:, p * n:(p + 1) * n] = l0
            l_out[:, (2 + p) * n:(3 + p) * n] = l1
        d0 = panel[:, :n].astype(BF)
        k0 = mm(d0, w2[0, 0]).astype(BF)
        d1 = (panel[:, n:] - mm_t(k0, lead_ref[...])).astype(BF)
        c_out[:, 2 * n:3 * n] = d0
        c_out[:, 3 * n:] = d1
        l_out[:, 4 * n:5 * n] = k0
        l_out[:, 5 * n:] = mm(d1, w2[0, 1]).astype(BF)

    def whole(v):
        return pl.BlockSpec(v.shape, lambda g, y: (0, 0))
    out = [jax.ShapeDtypeStruct((BLOCK, k * n), BF) for k in (4, 6)]
    return pl.pallas_call(
        body,
        out_shape=out,
        grid_spec=pltpu.PrefetchScalarGridSpec(
            num_scalar_prefetch=1,
            grid=(1,),
            in_specs=[
                whole(mine), whole(other),
                pl.BlockSpec((n, n), lambda g, y: (0, 0)),
                pl.BlockSpec((n, n), lambda g, y: (0, 2)),
                whole(lead[0]), whole(lead[1]),
                pl.BlockSpec((2, 2, n, n), lambda g, y: (y[1], 0, 0, 0)),
                pl.BlockSpec((1, 2, n, n), lambda g, y: (y[1], 0, 0, 0)),
            ] + [ANY] * len(earlier),
            out_specs=[whole(v) for v in out],
        ),
        cost_estimate=cost(3.5),
        compiler_params=params(),
    )(place, mine, other, special, special, *lead, w_one, w_two, *earlier)


def tile_update(parts, lower, first, columns, place):
    half = BLOCK // 2
    deep = first.shape[-1]

    def body(zs, *refs):
        part, head, l_refs, c_refs = refs[:2], refs[2:4], refs[4:4 + NX], refs[4 + NX:4 + NX + NZ]
        out, low = refs[-2:]

        @pl.when(pl.program_id(0) == 0)
        def _():
            for i in range(NX):
                low[pl.ds(pl.multiple_of((zs[1] + i) % NX * BLOCK, BLOCK), BLOCK), :] = l_refs[i][...]

        for step in range(NZ // 2):
            @pl.when(pl.program_id(0) == step)
            def _():
                c = jnp.concatenate([c_refs[2 * step][...], c_refs[2 * step + 1][...]], axis=0)
                update = mm_t(low[:, deep:], c) + mm_t(low[:, :deep], jnp.concatenate([head[0][0], head[1][0]], axis=0))
                for j in range(2):
                    for x in range(NX):
                        rows = slice(x * BLOCK, (x + 1) * BLOCK)
                        done = (part[j][x, 0].astype(F32) - update[rows, j * BLOCK:(j + 1) * BLOCK]).astype(BF)
                        out[x, j] = done[:half]
                        out[NX + x, j] = done[half:]

    def part_spec(j):
        return pl.BlockSpec((NX, 1, BLOCK, BLOCK), lambda g, s: (0, (s[0] + 2 * g + j) % NZ, 0, 0))

    def head_spec(j):
        return pl.BlockSpec((1, BLOCK, deep), lambda g, s: ((s[0] + 2 * g + j) % NZ, 0, 0))

    def whole(v):
        return pl.BlockSpec(v.shape, lambda g, s: (0, 0))
    return pl.pallas_call(
        body,
        out_shape=jax.ShapeDtypeStruct((2 * NX, NZ, half, BLOCK), BF),
        grid_spec=pltpu.PrefetchScalarGridSpec(
            num_scalar_prefetch=1,
            grid=(NZ // 2,),
            in_specs=[part_spec(0), part_spec(1), head_spec(0), head_spec(1)] + [whole(v) for v in (*lower, *columns)],
            out_specs=pl.BlockSpec((2 * NX, 2, half, BLOCK), lambda g, s: (0, g, 0, 0)),
            scratch_shapes=[pltpu.VMEM((NX * BLOCK, lower[0].shape[1]), BF)],
        ),
        cost_estimate=cost(7),
        compiler_params=params(LARGE),
    )(place, parts, parts, first, first, *lower, *columns)


def join_rows(pieces, place):
    half = BLOCK // 2
    wide = 2 * NX * BLOCK
    some = NZ // 2

    def body(zs, *refs):
        for i in range(some):
            for k in range(2):
                for x in range(NX):
                    c = i * wide + (2 * x + k) * BLOCK
                    refs[-1][:, c:c + BLOCK] = refs[i][k * NX + x, 0]

    def where_from(i):
        return lambda g, s: (0, (g * some + i + NZ - s[0]) % NZ, 0, 0)
    return pl.pallas_call(
        body,
        out_shape=jax.ShapeDtypeStruct((half, NB * BLOCK), BF),
        grid_spec=pltpu.PrefetchScalarGridSpec(
            num_scalar_prefetch=1,
            grid=(NZ // some,),
            in_specs=[pl.BlockSpec((2 * NX, 1, half, BLOCK), where_from(i)) for i in range(some)],
            out_specs=pl.BlockSpec((half, some * wide), lambda g, s: (0, g)),
        ),
        cost_estimate=cost(2.2),
        compiler_params=params(),
    )(place, *[pieces] * some)


def local(child_blocks, child_map, merged_map, pivots_one, pivots_two):
    q, yp, e = lax.axis_index("q"), lax.axis_index("yp"), lax.axis_index("core")
    z, x = lax.axis_index("z"), lax.axis_index("x")
    child = (q * 2 + yp) * 2 + e
    spot = z * NX + x
    slab = child_blocks[0].reshape(NB, BLOCK, 2 * BLOCK)
    source, filled, pivot_places = block_maps(child_map[child], merged_map[child // 2])

    own_filled = lax.dynamic_slice_in_dim(filled, 2 * spot, 2)
    lead_filled = filled[:4]
    panel_src = onehot_pick(source, jnp.concatenate([pivot_places, jnp.arange(4, dtype=jnp.int32)]))
    col_ok = jnp.concatenate([jnp.ones((4,), jnp.int32), lead_filled])

    row_src = onehot_pick(source, jnp.concatenate([pivot_places[2:], jnp.arange(4, dtype=jnp.int32)]))
    few = 6 * BLOCK // (NZ * NX)
    first = pick_rows(slab, row_src).reshape(NZ * NX, few, 2 * BLOCK)
    first = lax.all_to_all(first, ("z", "x"), split_axis=0, concat_axis=0, tiled=True)
    part_of = (spot * few + jnp.arange(few, dtype=jnp.int32)) // BLOCK
    row_ok = onehot_pick(jnp.concatenate([jnp.ones((2,), jnp.int32), lead_filled]), part_of)
    first = few_blocks(first, panel_src)
    first_ok = (row_ok[:, None] * jnp.repeat(col_ok, BLOCK)[None, :6 * BLOCK]) > 0
    first = jnp.where(first_ok, first, jnp.zeros_like(first))
    first = (first.astype(F32) + flip(first, "core").astype(F32)).astype(BF)
    second = flip(first, "yp")
    low = jnp.where(yp == 0, first, second)
    high = jnp.where(yp == 0, second, first)
    lead = (low[:, 2 * PANEL:].astype(F32) + high[:, 2 * PANEL:].astype(F32)).astype(BF)
    special = jnp.concatenate([low[:, :2 * PANEL], high[:, :2 * PANEL], lead], axis=1)
    special = lax.all_gather(special, ("z", "x"), axis=0, tiled=True)

    sent = slab.at[source].get(mode="promise_in_bounds").reshape(NZ * NX, 2 * BLOCK, 2 * BLOCK)
    rows = lax.all_to_all(sent, ("z", "x"), split_axis=0, concat_axis=0, tiled=True)

    panel_ok = (col_ok[:, None] * own_filled[None, :]).reshape(-1)
    core = e.reshape(1)
    tile_ok = (filled[:, None] * own_filled[None, :]).reshape(-1)
    group = jnp.stack([yp, q])
    lead = lead_rows(special, pivots_one, group)
    keep, send = panel_blocks(rows, panel_src, panel_ok, core, *lead)
    got = flip(send, "core")
    mine = (keep.astype(F32) + got.astype(F32)).astype(BF)
    other = flip(mine, "yp")
    tile_got = flip(tie((core_send(rows, source, core, keep),), got)[0], "core")
    first = jnp.concatenate([
        jnp.where(yp == 0, mine, other)[:, :PANEL], jnp.where(yp == 0, other, mine)[:, :PANEL]], axis=1)
    first = lax.all_gather(first, "z", axis=0, tiled=False)
    own, theirs = core_sum(rows, tile_got, source, tile_ok, jnp.stack([e, yp]))
    columns, lower = factor_rows(mine, other, special, lead, pivots_one, pivots_two, group, own)

    place = jnp.stack([z, x])
    z1 = tie(both_ways((columns, columns), "z", NZ))
    mate = flip(lower, "core")
    lower = jnp.where(e == yp, lower, mate)
    x1 = tie(both_ways((lower, lower), "x", NX))
    parts = (own.astype(F32) + flip(theirs, "yp").astype(F32)).astype(BF)
    x2 = shift(x1[0], "x", 1, NX)
    parts = lax.all_to_all(parts, "x", split_axis=0, concat_axis=0, tiled=True)
    z2 = tie(both_ways(z1, "z", NZ))
    z3 = tie(both_ways(z2, "z", NZ))
    z4 = shift(z3[0], "z", 1, NZ)
    lower = (lower, x1[1], x2, x1[0])

    columns = (columns, z1[1], z2[1], z3[1], z4, z3[0], z2[0], z1[0])
    done = tile_update(parts, lower, first, columns, place)
    done = lax.all_to_all(done, ("core", "x"), split_axis=0, concat_axis=0, tiled=True)
    return join_rows(done, place)[None, None]


def solution(mesh):
    fine = Mesh(mesh.devices.reshape(2, 2, 2, NZ, NX), ("q", "yp", "core", "z", "x"))
    leaf, plane = ("q", "yp", "core"), ("z", "x")
    return jax.shard_map(
        local,
        mesh=fine,
        in_specs=(P(leaf, None, plane), P(), P(), P(), P()),
        out_specs=P(plane, leaf, None, None),
        check_vma=False,
    )
```

```python
import jax
import jax.numpy as jnp
from jax import lax
from jax.experimental import pallas as pl
from jax.experimental.pallas import tpu as pltpu
from jax.sharding import Mesh, PartitionSpec as P

BLOCK = 128
PANEL = 256
NB = 64
NZ = 8
NX = 4
HALF = NB // 2
BF = jnp.bfloat16
F32 = jnp.float32
VMEM = 24 * 1024 * 1024
LARGE = 56 * 1024 * 1024


def params(limit=VMEM):
    return pltpu.CompilerParams(vmem_limit_bytes=limit)


def cost(us):
    return pl.CostEstimate(flops=0, bytes_accessed=int(us * 3.6e5), transcendentals=0)


def shift(v, axis, step, n):
    return lax.ppermute(v, axis, [(i, (i + step) % n) for i in range(n)])


def flip(v, axis):
    return lax.ppermute(v, axis, [(0, 1), (1, 0)])


ANY = pl.BlockSpec(memory_space=pl.ANY)


def tie(values, *earlier):
    n = len(values)
    return pl.pallas_call(
        lambda *refs: None,
        out_shape=tuple(jax.ShapeDtypeStruct(v.shape, v.dtype) for v in values),
        in_specs=[ANY] * (n + len(earlier)),
        out_specs=(ANY,) * n,
        cost_estimate=cost(0.5),
        input_output_aliases={i: i for i in range(n)},
    )(*values, *earlier)


def both_ways(pair, axis, n):
    return shift(pair[0], axis, 1, n), shift(pair[1], axis, -1, n)


def onehot_pick(table, index):
    hit = index[:, None] == jnp.arange(table.shape[0], dtype=jnp.int32)[None, :]
    return jnp.sum(jnp.where(hit, table[None, :], 0), axis=1).astype(jnp.int32)


def block_maps(child_row, merged_row):
    target = jnp.arange(NB, dtype=jnp.int32)
    hits = merged_row[None, :] == target[:, None]
    filled = jnp.any(hits, axis=1)
    place = jnp.sum(jnp.where(hits, jnp.arange(merged_row.shape[0], dtype=jnp.int32)[None, :] + 4, 0), axis=1)
    before = target[None, :] < target[:, None]
    rank = jnp.sum(jnp.where(before & ~filled[None, :], 1, 0), axis=1)
    first_index = jnp.where(filled, place, rank).astype(jnp.int32)
    child_hits = child_row[None, :] == first_index[:, None]
    source = jnp.sum(jnp.where(child_hits, target[None, :], 0), axis=1).astype(jnp.int32)
    wanted = jnp.arange(4, dtype=jnp.int32)
    pivot = (~filled)[None, :] & (rank[None, :] == wanted[:, None])
    pivot_places = jnp.sum(jnp.where(pivot, target[None, :], 0), axis=1).astype(jnp.int32)
    return source, filled.astype(jnp.int32), pivot_places


def panel_blocks(rows, source, ok, core, *earlier):
    def body(src, okr, ce, *refs):
        e = ce[0]
        for i in range(8):
            for out, r in ((refs[-2], e), (refs[-1], 1 - e)):
                part = refs[i][0, pl.ds(pl.multiple_of(r * BLOCK, BLOCK), BLOCK), :]
                out[:, i * BLOCK:(i + 1) * BLOCK] = jnp.where(okr[i * 2 + r] > 0, part, jnp.zeros_like(part))

    def where_from(i):
        return lambda g, s, o, c: (s[i] // 2, 0, s[i] % 2)
    one = jax.ShapeDtypeStruct((BLOCK, 8 * BLOCK), BF)
    return pl.pallas_call(
        body,
        out_shape=(one, one),
        grid_spec=pltpu.PrefetchScalarGridSpec(
            num_scalar_prefetch=3,
            grid=(1,),
            in_specs=[pl.BlockSpec((1, 2 * BLOCK, BLOCK), where_from(i)) for i in range(8)] + [ANY] * len(earlier),
            out_specs=[pl.BlockSpec((BLOCK, 8 * BLOCK), lambda g, s, o, c: (0, 0))] * 2,
        ),
        cost_estimate=cost(1.8),
        compiler_params=params(),
    )(source, ok, core, *[rows] * 8, *earlier)


def core_send(rows, source, core, *earlier):
    def body(src, ce, rows_ref, *refs):
        far, held, sems, out_sems = refs[-4:]
        ins, outs = [], []
        for x in range(NX):
            for z in range(NZ):
                b = src[2 * (z * NX + x) + 1 - ce[0]]
                lanes = pl.ds(pl.multiple_of(b % 2 * BLOCK, BLOCK), BLOCK)
                ins.append(pltpu.make_async_copy(rows_ref.at[b // 2, :, lanes], held.at[x, z], sems.at[x, z]))
                ins[-1].start()
        for x in range(NX):
            for z in range(NZ):
                ins[x * NZ + z].wait()
            outs.append(pltpu.make_async_copy(held.at[x], far.at[x], out_sems.at[x]))
            outs[-1].start()
        for move in outs:
            move.wait()

    shape = (NX, NZ, 2 * BLOCK, BLOCK)
    return pl.pallas_call(
        body,
        out_shape=jax.ShapeDtypeStruct(shape, BF),
        grid_spec=pltpu.PrefetchScalarGridSpec(
            num_scalar_prefetch=2,
            grid=(1,),
            in_specs=[ANY] * (1 + len(earlier)),
            out_specs=ANY,
            scratch_shapes=[
                pltpu.VMEM(shape, BF),
                pltpu.SemaphoreType.DMA((NX, NZ)),
                pltpu.SemaphoreType.DMA((NX,)),
            ],
        ),
        cost_estimate=cost(3.3),
        compiler_params=params(),
    )(source, core, rows, *earlier)


def pick_rows(slab, source):
    n = source.shape[0]

    def body(src, *refs):
        for i in range(n):
            refs[-1][i] = refs[i][0]
    shape = (n,) + slab.shape[1:]

    def where_from(i):
        return lambda g, s: (s[i], 0, 0)
    return pl.pallas_call(
        body,
        out_shape=jax.ShapeDtypeStruct(shape, BF),
        grid_spec=pltpu.PrefetchScalarGridSpec(
            num_scalar_prefetch=1,
            grid=(1,),
            in_specs=[pl.BlockSpec((1,) + slab.shape[1:], where_from(i)) for i in range(n)],
            out_specs=pl.BlockSpec(shape, lambda g, s: (0, 0, 0)),
        ),
        cost_estimate=cost(1.3),
        compiler_params=params(LARGE),
    )(source, *[slab] * n)


def few_blocks(rows, source):
    few = rows.shape[1]

    def body(src, *refs):
        for i in range(6):
            refs[-1][:, i * BLOCK:(i + 1) * BLOCK] = refs[i][0]

    def where_from(i):
        return lambda g, s: (s[i] // 2, 0, s[i] % 2)
    return pl.pallas_call(
        body,
        out_shape=jax.ShapeDtypeStruct((few, 6 * BLOCK), BF),
        grid_spec=pltpu.PrefetchScalarGridSpec(
            num_scalar_prefetch=1,
            grid=(1,),
            in_specs=[pl.BlockSpec((1, few, BLOCK), where_from(i)) for i in range(6)],
            out_specs=pl.BlockSpec((few, 6 * BLOCK), lambda g, s: (0, 0)),
        ),
        cost_estimate=cost(0.6),
        compiler_params=params(),
    )(source, *[rows] * 6)


STEP = NZ


def column_specs(core_of):
    def where_from(i):
        def index(x, w, s, o, c):
            b = s[2 * ((w * STEP + i) * NX + x) + core_of(c[0])]
            return (b // 2, 0, b % 2)
        return index
    return [pl.BlockSpec((1, 2 * BLOCK, BLOCK), where_from(i)) for i in range(STEP)]


def core_sum(rows, got, source, ok, place):
    def body(src, okr, ce, *refs):
        x, w = pl.program_id(0), pl.program_id(1)
        keep, send = refs[-2:]
        for i in range(STEP):
            c = 2 * ((w * STEP + i) * NX + x) + ce[0]
            for out, r in ((keep, ce[1]), (send, 1 - ce[1])):
                part = pl.ds(pl.multiple_of(r * BLOCK, BLOCK), BLOCK)
                total = (refs[i][0, part, :].astype(F32) + refs[STEP][0, i, part, :].astype(F32)).astype(BF)
                out[0, i] = jnp.where(okr[c * 2 + r] > 0, total, jnp.zeros_like(total))

    one = jax.ShapeDtypeStruct((NX, NZ, BLOCK, BLOCK), BF)
    return pl.pallas_call(
        body,
        out_shape=(one, one),
        grid_spec=pltpu.PrefetchScalarGridSpec(
            num_scalar_prefetch=3,
            grid=(NX, NZ // STEP),
            in_specs=column_specs(lambda e: e) + [
                pl.BlockSpec((1, STEP, 2 * BLOCK, BLOCK), lambda x, w, s, o, c: (x, w, 0, 0))],
            out_specs=[pl.BlockSpec((1, STEP, BLOCK, BLOCK), lambda x, w, s, o, c: (x, w, 0, 0))] * 2,
        ),
        cost_estimate=cost(4.2),
        compiler_params=params(),
    )(source, ok, place, *[rows] * STEP, got)


def mm(a, b):
    return jnp.dot(a, b, preferred_element_type=F32)


def mm_t(a, b):
    return lax.dot_general(a, b, (((1,), (1,)), ((), ())), preferred_element_type=F32)


def lead_rows(special, w_one, place):
    n = PANEL

    def body(y, s_ref, w1, t_out, lead_out):
        lead = s_ref[2 * n:, 4 * n:].astype(F32)
        for p in range(2):
            low = slice(2 * p * n, (2 * p + 1) * n)
            high = slice((2 * p + 1) * n, (2 * p + 2) * n)
            t0 = s_ref[n:, low]
            l0 = mm(t0, w1[p, 0]).astype(BF)
            t1 = (s_ref[n:, high].astype(F32) - mm_t(l0, s_ref[:n, low])).astype(BF)
            l1 = mm(t1[n:], w1[p, 1]).astype(BF)
            lead = lead - mm_t(l0[n:], t0[:n]) - mm_t(l1, t1[:n])
            t_out[:, low] = t0
            t_out[:, high] = t1
        lead_out[...] = lead.astype(BF)

    def whole(v):
        return pl.BlockSpec(v.shape, lambda g, y: (0, 0))
    out = jax.ShapeDtypeStruct((2 * n, 4 * n), BF), jax.ShapeDtypeStruct((n, n), BF)
    return pl.pallas_call(
        body,
        out_shape=out,
        grid_spec=pltpu.PrefetchScalarGridSpec(
            num_scalar_prefetch=1,
            grid=(1,),
            in_specs=[whole(special), pl.BlockSpec((2, 2, n, n), lambda g, y: (y[1], 0, 0, 0))],
            out_specs=[whole(v) for v in out],
        ),
        cost_estimate=cost(1.6),
        compiler_params=params(),
    )(place, special, w_one)


def factor_rows(mine, other, special, lead, w_one, w_two, place, *earlier):
    n = PANEL

    def body(y, a_ref, b_ref, p0, p1, t_ref, lead_ref, w1, w2, *refs):
        c_out, l_out, first_out = refs[-3:]
        first = y[0] == 0
        a, b = a_ref[...], b_ref[...]
        both = (jnp.where(first, a, b), jnp.where(first, b, a))
        panel = (a[:, 2 * n:].astype(F32) + b[:, 2 * n:].astype(F32)).astype(BF).astype(F32)
        for p in range(2):
            low = slice(2 * p * n, (2 * p + 1) * n)
            high = slice((2 * p + 1) * n, (2 * p + 2) * n)
            c0 = both[p][:, :n]
            l0 = mm(c0, w1[p, 0]).astype(BF)
            c1 = (both[p][:, n:2 * n].astype(F32) - mm_t(l0, (p0, p1)[p][...])).astype(BF)
            l1 = mm(c1, w1[p, 1]).astype(BF)
            panel = panel - mm_t(l0, t_ref[:, low]) - mm_t(l1, t_ref[:, high])
            first_out[:, p * n:(p + 1) * n] = c0
            c_out[:, p * n:(p + 1) * n] = c1
            l_out[:, p * n:(p + 1) * n] = l0
            l_out[:, (2 + p) * n:(3 + p) * n] = l1
        d0 = panel[:, :n].astype(BF)
        k0 = mm(d0, w2[0, 0]).astype(BF)
        d1 = (panel[:, n:] - mm_t(k0, lead_ref[...])).astype(BF)
        c_out[:, 2 * n:3 * n] = d0
        c_out[:, 3 * n:] = d1
        l_out[:, 4 * n:5 * n] = k0
        l_out[:, 5 * n:] = mm(d1, w2[0, 1]).astype(BF)

    def whole(v):
        return pl.BlockSpec(v.shape, lambda g, y: (0, 0))
    out = [jax.ShapeDtypeStruct((BLOCK, k * n), BF) for k in (4, 6, 2)]
    return pl.pallas_call(
        body,
        out_shape=out,
        grid_spec=pltpu.PrefetchScalarGridSpec(
            num_scalar_prefetch=1,
            grid=(1,),
            in_specs=[
                whole(mine), whole(other),
                pl.BlockSpec((n, n), lambda g, y: (0, 0)),
                pl.BlockSpec((n, n), lambda g, y: (0, 2)),
                whole(lead[0]), whole(lead[1]),
                pl.BlockSpec((2, 2, n, n), lambda g, y: (y[1], 0, 0, 0)),
                pl.BlockSpec((1, 2, n, n), lambda g, y: (y[1], 0, 0, 0)),
            ] + [ANY] * len(earlier),
            out_specs=[whole(v) for v in out],
        ),
        cost_estimate=cost(3.5),
        compiler_params=params(),
    )(place, mine, other, special, special, *lead, w_one, w_two, *earlier)


def tile_update(parts, lower, first, columns, place):
    half = BLOCK // 2
    deep = first.shape[-1]

    def body(zs, *refs):
        part, head, l_refs, c_refs = refs[:2], refs[2:4], refs[4:4 + NX], refs[4 + NX:4 + NX + NZ]
        out, low = refs[-2:]

        @pl.when(pl.program_id(0) == 0)
        def _():
            for i in range(NX):
                low[pl.ds(pl.multiple_of((zs[1] + i) % NX * BLOCK, BLOCK), BLOCK), :] = l_refs[i][...]

        for step in range(NZ // 2):
            @pl.when(pl.program_id(0) == step)
            def _():
                c = jnp.concatenate([c_refs[2 * step][...], c_refs[2 * step + 1][...]], axis=0)
                update = mm_t(low[:, deep:], c) + mm_t(low[:, :deep], jnp.concatenate([head[0][0], head[1][0]], axis=0))
                for j in range(2):
                    for x in range(NX):
                        rows = slice(x * BLOCK, (x + 1) * BLOCK)
                        done = (part[j][x, 0].astype(F32) - update[rows, j * BLOCK:(j + 1) * BLOCK]).astype(BF)
                        out[x, j] = done[:half]
                        out[NX + x, j] = done[half:]

    def part_spec(j):
        return pl.BlockSpec((NX, 1, BLOCK, BLOCK), lambda g, s: (0, (s[0] + 2 * g + j) % NZ, 0, 0))

    def head_spec(j):
        return pl.BlockSpec((1, BLOCK, deep), lambda g, s: ((s[0] + 2 * g + j) % NZ, 0, 0))

    def whole(v):
        return pl.BlockSpec(v.shape, lambda g, s: (0, 0))
    return pl.pallas_call(
        body,
        out_shape=jax.ShapeDtypeStruct((2 * NX, NZ, half, BLOCK), BF),
        grid_spec=pltpu.PrefetchScalarGridSpec(
            num_scalar_prefetch=1,
            grid=(NZ // 2,),
            in_specs=[part_spec(0), part_spec(1), head_spec(0), head_spec(1)] + [whole(v) for v in (*lower, *columns)],
            out_specs=pl.BlockSpec((2 * NX, 2, half, BLOCK), lambda g, s: (0, g, 0, 0)),
            scratch_shapes=[pltpu.VMEM((NX * BLOCK, lower[0].shape[1]), BF)],
        ),
        cost_estimate=cost(7),
        compiler_params=params(LARGE),
    )(place, parts, parts, first, first, *lower, *columns)


def join_rows(pieces, place):
    half = BLOCK // 2
    wide = 2 * NX * BLOCK
    some = NZ // 2

    def body(zs, *refs):
        for i in range(some):
            for k in range(2):
                for x in range(NX):
                    c = i * wide + (2 * x + k) * BLOCK
                    refs[-1][:, c:c + BLOCK] = refs[i][k * NX + x, 0]

    def where_from(i):
        return lambda g, s: (0, (g * some + i + NZ - s[0]) % NZ, 0, 0)
    return pl.pallas_call(
        body,
        out_shape=jax.ShapeDtypeStruct((half, NB * BLOCK), BF),
        grid_spec=pltpu.PrefetchScalarGridSpec(
            num_scalar_prefetch=1,
            grid=(NZ // some,),
            in_specs=[pl.BlockSpec((2 * NX, 1, half, BLOCK), where_from(i)) for i in range(some)],
            out_specs=pl.BlockSpec((half, some * wide), lambda g, s: (0, g)),
        ),
        cost_estimate=cost(2.2),
        compiler_params=params(),
    )(place, *[pieces] * some)


def local(child_blocks, child_map, merged_map, pivots_one, pivots_two):
    q, yp, e = lax.axis_index("q"), lax.axis_index("yp"), lax.axis_index("core")
    z, x = lax.axis_index("z"), lax.axis_index("x")
    child = (q * 2 + yp) * 2 + e
    spot = z * NX + x
    slab = child_blocks[0].reshape(NB, BLOCK, 2 * BLOCK)
    source, filled, pivot_places = block_maps(child_map[child], merged_map[child // 2])

    own_filled = lax.dynamic_slice_in_dim(filled, 2 * spot, 2)
    lead_filled = filled[:4]
    panel_src = onehot_pick(source, jnp.concatenate([pivot_places, jnp.arange(4, dtype=jnp.int32)]))
    col_ok = jnp.concatenate([jnp.ones((4,), jnp.int32), lead_filled])

    row_src = onehot_pick(source, jnp.concatenate([pivot_places[2:], jnp.arange(4, dtype=jnp.int32)]))
    few = 6 * BLOCK // (NZ * NX)
    first = pick_rows(slab, row_src).reshape(NZ * NX, few, 2 * BLOCK)
    first = lax.all_to_all(first, ("z", "x"), split_axis=0, concat_axis=0, tiled=True)
    part_of = (spot * few + jnp.arange(few, dtype=jnp.int32)) // BLOCK
    row_ok = onehot_pick(jnp.concatenate([jnp.ones((2,), jnp.int32), lead_filled]), part_of)
    first = few_blocks(first, panel_src)
    first_ok = (row_ok[:, None] * jnp.repeat(col_ok, BLOCK)[None, :6 * BLOCK]) > 0
    first = jnp.where(first_ok, first, jnp.zeros_like(first))
    first = (first.astype(F32) + flip(first, "core").astype(F32)).astype(BF)
    second = flip(first, "yp")
    low = jnp.where(yp == 0, first, second)
    high = jnp.where(yp == 0, second, first)
    lead = (low[:, 2 * PANEL:].astype(F32) + high[:, 2 * PANEL:].astype(F32)).astype(BF)
    special = jnp.concatenate([low[:, :2 * PANEL], high[:, :2 * PANEL], lead], axis=1)
    special = lax.all_gather(special, ("z", "x"), axis=0, tiled=True)

    sent = slab.at[source].get(mode="promise_in_bounds").reshape(NZ * NX, 2 * BLOCK, 2 * BLOCK)
    rows = lax.all_to_all(sent, ("z", "x"), split_axis=0, concat_axis=0, tiled=True)

    panel_ok = (col_ok[:, None] * own_filled[None, :]).reshape(-1)
    core = e.reshape(1)
    tile_ok = (filled[:, None] * own_filled[None, :]).reshape(-1)
    group = jnp.stack([yp, q])
    lead = lead_rows(special, pivots_one, group)
    keep, send = panel_blocks(rows, panel_src, panel_ok, core, *lead)
    got = flip(send, "core")
    mine = (keep.astype(F32) + got.astype(F32)).astype(BF)
    other = flip(mine, "yp")
    tile_got = flip(tie((core_send(rows, source, core, keep),), got)[0], "core")
    own, theirs = core_sum(rows, tile_got, source, tile_ok, jnp.stack([e, yp]))
    columns, lower, first = factor_rows(mine, other, special, lead, pivots_one, pivots_two, group, own)

    first = lax.all_gather(first, "z", axis=0, tiled=False)

    place = jnp.stack([z, x])
    z1 = tie(both_ways((columns, columns), "z", NZ))
    mate = flip(lower, "core")
    lower = jnp.where(e == yp, lower, mate)
    x1 = tie(both_ways((lower, lower), "x", NX))
    parts = (own.astype(F32) + flip(theirs, "yp").astype(F32)).astype(BF)
    x2 = shift(x1[0], "x", 1, NX)
    parts = lax.all_to_all(parts, "x", split_axis=0, concat_axis=0, tiled=True)
    z2 = tie(both_ways(z1, "z", NZ))
    z3 = tie(both_ways(z2, "z", NZ))
    z4 = shift(z3[0], "z", 1, NZ)
    lower = (lower, x1[1], x2, x1[0])

    columns = (columns, z1[1], z2[1], z3[1], z4, z3[0], z2[0], z1[0])
    done = tile_update(parts, lower, first, columns, place)
    done = lax.all_to_all(done, ("core", "x"), split_axis=0, concat_axis=0, tiled=True)
    return join_rows(done, place)[None, None]


def solution(mesh):
    fine = Mesh(mesh.devices.reshape(2, 2, 2, NZ, NX), ("q", "yp", "core", "z", "x"))
    leaf, plane = ("q", "yp", "core"), ("z", "x")
    return jax.shard_map(
        local,
        mesh=fine,
        in_specs=(P(leaf, None, plane), P(), P(), P(), P()),
        out_specs=P(plane, leaf, None, None),
        check_vma=False,
    )
```
